32 devices in a mesh: seq: 8 (over z, y), wshard: 4 (over x, core).
Axes of the slice: x: 2, y: 2, z: 4, core: 2. Of those that a mesh axis runs over, the one named last changes fastest.
Arguments:
- inputs: bfloat16 [4, 8192, 768], P('wshard', 'seq'), may hold values from -6 to 6
- gain_attn: bfloat16 [768], P('wshard'), may hold values from 0.5 to 1.5
- w_qkv: bfloat16 [768, 2304], P('wshard'), may hold values from -0.21875 to 0.21875
- w_out: bfloat16 [768, 768], P('wshard'), may hold values from -1.25 to 1.25
- gain_mlp: bfloat16 [768], P('wshard'), may hold values from 0.5 to 1.5
- w_in: bfloat16 [768, 2304], P('wshard'), may hold values from -0.21875 to 0.21875
- w_down: bfloat16 [1152, 768], P('wshard'), may hold values from -0.1875 to 0.1875
- bounds: int32 [4, 2], P('wshard'), may hold values from 1 to 8191, as said below
- grad_out: bfloat16 [4, 8192, 768], P('wshard', 'seq'), may hold values from -6 to 6
Outputs:
- output: bfloat16 [4, 8192, 768], P('wshard', 'seq')
- input_grad: bfloat16 [4, 8192, 768], P('wshard', 'seq')
- gain_attn_grad: float32 [768], P('wshard')
- w_qkv_grad: float32 [768, 2304], P('wshard')
- w_out_grad: float32 [768, 768], P('wshard')
- gain_mlp_grad: float32 [768], P('wshard')
- w_in_grad: float32 [768, 2304], P('wshard')
- w_down_grad: float32 [1152, 768], P('wshard')
The draws below stay inside these ranges and needn't reach their ends.
Inputs may be any that keep to these rules, and one draw needn't show every extreme that they name: `bounds`: each sequence packs three documents: the second begins within its first 1024 tokens (column 0) and the third within its last 1024 tokens (column 1).
All inputs are finite; a program needn't handle non-finite values.
Results may differ from the reference program's by a relative error of at most 0.02.
Values may be sent and summed in bfloat16 or wider, within the bound.
A program may use at most 192 MiB of HBM per device.

```python
import math
import jax
import jax.numpy as jnp
from jax import lax

D = 768
HD = 64
FF = 1152
HALF = 64
TOK_DEV = 1024
LEN = 8192
SEQS = 4


def draw_bounds(key, part):
    key = jax.random.fold_in(key, 11)
    first_key, last_key, pick_key = jax.random.split(key, 3)
    first_cut = jax.random.randint(first_key, (SEQS, 1), 1, TOK_DEV, dtype=jnp.int32)
    last_cut = LEN - jax.random.randint(last_key, (SEQS, 1), 1, TOK_DEV, dtype=jnp.int32)
    picks = jax.random.randint(pick_key, (2,), 0, SEQS, dtype=jnp.int32)
    rows = jnp.arange(SEQS, dtype=jnp.int32)[:, None]
    first_cut = jnp.where(rows == picks[0], jnp.int32(1), first_cut)
    last_cut = jnp.where(rows == picks[1], jnp.int32(LEN - 1), last_cut)
    return jnp.concatenate([first_cut, last_cut], axis=1)


def level_of(own_key, extent, cuts, smallest, largest):
    factor_of = 1.0
    for dim, blocks in cuts:
        heights = jax.random.uniform(jax.random.fold_in(jax.random.fold_in(own_key, 6), dim), (blocks,), jnp.float32, smallest / len(cuts), largest / len(cuts))
        factor_of = factor_of * jnp.repeat(jnp.exp(heights), extent[dim] // blocks).reshape((-1,) + (1,) * (len(extent) - 1 - dim))
    return factor_of


def gaussian(key, extent, scale, most, shards=(), kind=jnp.bfloat16):
    loudness = level_of(key, extent, shards, -0.22, 0.18) if shards else 1.0
    array = jax.random.normal(key, extent, jnp.float32) * scale * loudness
    return jnp.minimum(jnp.maximum(array, -most), most).astype(kind)


def setup_inputs(seed: int = 0) -> dict:
    seeds = jax.random.split(jax.random.key(seed), 10)
    return {
        "inputs": gaussian(seeds[0], (SEQS, LEN, D), 1.0, 6.0, ((0, 4), (1, 8))),
        "gain_attn": jnp.clip(1.0 + 0.1 * jax.random.normal(seeds[1], (D,), jnp.float32), 0.5, 1.5).astype(jnp.bfloat16),
        "w_qkv": gaussian(seeds[2], (D, 3 * D), D ** -0.5, 0.21875, ((0, 4),)),
        "w_out": gaussian(seeds[3], (D, D), (D // 32) ** -0.5, 1.25, ((0, 4),)),
        "gain_mlp": jnp.clip(1.0 + 0.1 * jax.random.normal(seeds[4], (D,), jnp.float32), 0.5, 1.5).astype(jnp.bfloat16),
        "w_in": gaussian(seeds[5], (D, 2 * FF), D ** -0.5, 0.21875, ((0, 4),)),
        "w_down": gaussian(seeds[6], (FF, D), FF ** -0.5, 0.1875, ((0, 4),)),
        "bounds": draw_bounds(jax.random.fold_in(seeds[9], 71), 0),
        "grad_out": gaussian(seeds[8], (SEQS, LEN, D), 1.0, 6.0, ((0, 4), (1, 8))),
    }


highest = lax.Precision.HIGHEST
rope_base = 10000.0

@jax.custom_vjp
def low(v):
    return lax.optimization_barrier(v.astype(jnp.bfloat16)).astype(jnp.float32)

@jax.custom_vjp
def low_back(v):
    return v

def low_keep(v):
    return (low(v), None)

def low_pass(kept, grad):
    return (grad,)

def back_keep(v):
    return (v, None)

def back_low(kept, grad):
    return (low(grad),)
low.defvjp(low_keep, low_pass)
low_back.defvjp(back_keep, back_low)

def layer_norm(stream, gain):
    centred = stream - lax.optimization_barrier(jnp.mean(stream, axis=-1, keepdims=True))
    spread = lax.optimization_barrier(jnp.mean(centred * centred, axis=-1, keepdims=True))
    return centred * lax.rsqrt(spread + 1e-05) * gain

def rope_tables(positions, head_dim):
    frequency = rope_base ** (-(jnp.arange(head_dim // 2, dtype=jnp.float32) * 2.0) / head_dim)
    angles = positions[:, None] * frequency[None, :]
    return (jnp.cos(angles)[:, None, :], jnp.sin(angles)[:, None, :])

def rotary(tensor, cosine, sine_table):
    half_dim = tensor.shape[-1] // 2
    upper_half = tensor[..., :half_dim]
    lower_half = tensor[..., half_dim:]
    return jnp.concatenate([upper_half * cosine - lower_half * sine_table, lower_half * cosine + upper_half * sine_table], axis=-1)

def key_mask(query_pos, key_pos, cut_first, cut_last, length):

    def segment(where_at):
        return (where_at >= cut_first).astype(jnp.int32) + (where_at >= cut_last).astype(jnp.int32)
    nearby = jnp.abs(query_pos[:, None] - key_pos[None, :]) <= HALF
    inside = (key_pos >= 0) & (key_pos < length)
    return nearby & inside[None, :] & (segment(query_pos)[:, None] == segment(key_pos)[None, :])

def attend(query, key_all, value_all, cut_first, cut_last):
    length = query.shape[0]
    block_rows = math.gcd(length, 512)
    padded_k = jnp.pad(key_all, ((HALF, HALF), (0, 0), (0, 0)))
    padded_v = jnp.pad(value_all, ((HALF, HALF), (0, 0), (0, 0)))
    scale_factor = 1.0 / math.sqrt(query.shape[-1])

    def one_block(block_index):
        offset = block_index * block_rows
        query_block = lax.dynamic_slice_in_dim(query, offset, block_rows, 0)
        key_block = lax.dynamic_slice_in_dim(padded_k, offset, block_rows + 2 * HALF, 0)
        value_block = lax.dynamic_slice_in_dim(padded_v, offset, block_rows + 2 * HALF, 0)
        query_pos = offset + jnp.arange(block_rows, dtype=jnp.int32)
        key_pos = offset - HALF + jnp.arange(block_rows + 2 * HALF, dtype=jnp.int32)
        allowed = key_mask(query_pos, key_pos, cut_first, cut_last, length)
        scores = jnp.einsum('qhd,khd->hqk', query_block, key_block, precision=highest) * scale_factor
        scores = low_back(scores)
        scores = jnp.where(allowed[None], scores, -1e+30)
        weights = low(jax.nn.softmax(scores, axis=-1))
        return jnp.einsum('hqk,khd->qhd', weights, value_block, precision=highest)
    blocks_out = lax.map(jax.checkpoint(one_block), jnp.arange(length // block_rows, dtype=jnp.int32))
    return blocks_out.reshape(length, -1)

def layer(stream, gain_a, weight_qkv, weight_out, gain_m, weight_in, weight_down, cut_first, cut_last):
    length, model_width = stream.shape
    head_count = model_width // HD
    hidden_width = weight_down.shape[0]
    normed = low(layer_norm(stream, gain_a))
    projected = jnp.dot(normed, weight_qkv, precision=highest)
    query_raw = low_back(projected[:, :model_width]).reshape(length, head_count, HD)
    key_raw = low_back(projected[:, model_width:2 * model_width]).reshape(length, head_count, HD)
    values = low(low_back(projected[:, 2 * model_width:])).reshape(length, head_count, HD)
    cosine, sine_table = rope_tables(jnp.arange(length, dtype=jnp.float32), HD)
    query = low(low_back(rotary(query_raw, cosine, sine_table)))
    key_rot = low(low_back(rotary(key_raw, cosine, sine_table)))
    attended = low(low_back(attend(query, key_rot, values, cut_first, cut_last)))
    branch = low_back(jnp.dot(attended, weight_out, precision=highest))
    middle = stream + branch
    normed2 = low(layer_norm(middle, gain_m))
    lifted = low_back(jnp.dot(normed2, weight_in, precision=highest))
    hidden = low(jax.nn.gelu(lifted[:, :hidden_width], approximate=False) * lifted[:, hidden_width:])
    return middle + low_back(jnp.dot(hidden, weight_down, precision=highest))

def reference(inputs, gain_attn, w_qkv, w_out, gain_mlp, w_in, w_down, bounds, grad_out):
    params = tuple((weight.astype(jnp.float32) for weight in (gain_attn, w_qkv, w_out, gain_mlp, w_in, w_down)))

    def per_sequence(totals, entries):
        seq_in, seq_grad, cut_points = entries

        def forward(stream, *layer_params):
            return layer(stream, *layer_params, cut_points[0], cut_points[1])
        result, pullback = jax.vjp(forward, seq_in.astype(jnp.float32), *params)
        gradients = pullback(seq_grad.astype(jnp.float32))
        totals = tuple((total + gradient for total, gradient in zip(totals, gradients[1:])))
        return (totals, (result.astype(jnp.bfloat16), gradients[0].astype(jnp.bfloat16)))
    initial = tuple((jnp.zeros(weight.shape, jnp.float32) for weight in params))
    totals, (outputs, input_grads) = lax.scan(per_sequence, initial, (inputs, grad_out, bounds))
    return (outputs, input_grads, totals[0], totals[1], totals[2], totals[3], totals[4], totals[5])
```

```python
import math

import jax
import jax.numpy as jnp
from jax import lax
from jax.sharding import PartitionSpec as P

HD = 64
HALF = 64


rope_base = 10000.0


def extended_2(shard, sides, width):
    for axis, dim in sides:
        size, length = (lax.axis_size(axis), shard.shape[dim])
        up = [(i, (i + 1) % size) for i in range(size - 1)]
        down = [(j, i) for i, j in up]
        last = lax.slice_in_dim(shard, length - width, length, axis=dim)
        leading = lax.slice_in_dim(shard, 0, width, axis=dim)
        before = lax.ppermute(last, axis, up)
        after = lax.ppermute(leading, axis, down)
        shard = jnp.concatenate([before, shard, after], axis=dim)
    return shard


def from_behind(shard, axis, by):
    size = lax.axis_size(axis)
    pairs = [(i, i + by) for i in range(size) if 0 <= i + by < size]
    return lax.ppermute(shard, axis, pairs)


def swap(shard, axis, bit):
    return lax.ppermute(shard, axis, [(i, i ^ bit) for i in range(lax.axis_size(axis))])


def bits_of(axis):
    return [1 << b for b in range(lax.axis_size(axis).bit_length() - 1)]


def gathered_small(shard, axis):
    parts = shard[None]
    for bit in bits_of(axis):
        other = swap(parts, axis, bit)
        upper = (lax.axis_index(axis) & bit) > 0
        parts = jnp.concatenate(
            [jnp.where(upper, other, parts), jnp.where(upper, parts, other)], axis=0
        )
    return parts.reshape((-1,) + shard.shape[1:])


def reduced(term, owner_axis, sum_axis):
    for bit in bits_of(owner_axis):
        side = ((lax.axis_index(owner_axis) & bit) > 0).astype(jnp.int32)
        pairs = term.reshape((term.shape[0] // 2, 2) + term.shape[1:])
        kept = lax.dynamic_index_in_dim(pairs, side, 1, keepdims=False)
        sent = lax.dynamic_index_in_dim(pairs, 1 - side, 1, keepdims=False)
        term = kept + swap(sent, owner_axis, bit)
    total = term[0]
    halved = []
    bits = bits_of(sum_axis)
    for bit in bits:
        rows = total.shape[0]
        if bit != bits[-1] and rows % 32 == 0:
            side = ((lax.axis_index(sum_axis) & bit) > 0).astype(jnp.int32)
            kept = lax.dynamic_slice_in_dim(total, side * (rows // 2), rows // 2, 0)
            sent = lax.dynamic_slice_in_dim(total, (1 - side) * (rows // 2), rows // 2, 0)
            total = kept + swap(sent, sum_axis, bit)
            halved.append(bit)
        else:
            total = total + swap(total, sum_axis, bit)
    for bit in reversed(halved):
        other = swap(total, sum_axis, bit)
        upper = (lax.axis_index(sum_axis) & bit) > 0
        total = jnp.concatenate(
            [jnp.where(upper, other, total), jnp.where(upper, total, other)], axis=0
        )
    return total


def total_of(grad):
    owners = lax.axis_size("wshard")
    term = grad.astype(jnp.bfloat16).reshape(owners, grad.shape[0] // owners, grad.shape[1])
    return reduced(term, "wshard", "seq").astype(jnp.float32)


def layer_norm(stream, gain):
    centred = stream - jnp.mean(stream, axis=-1, keepdims=True)
    spread = jnp.mean(centred * centred, axis=-1, keepdims=True)
    return centred * lax.rsqrt(spread + 1e-05) * gain


def gated_act(lifted):
    hidden_width = lifted.shape[1] // 2
    return jax.nn.gelu(lifted[:, :hidden_width], approximate=False) * lifted[:, hidden_width:]


def rope_tables(positions, head_dim):
    frequency = rope_base ** (-(jnp.arange(head_dim // 2, dtype=jnp.float32) * 2.0) / head_dim)
    angles = positions[:, None] * frequency[None, :]
    return (jnp.cos(angles)[:, None, :], jnp.sin(angles)[:, None, :])


def rotate(tensor, cosine, sine_table, direction):
    half_dim = tensor.shape[-1] // 2
    upper_half = tensor[..., :half_dim]
    lower_half = tensor[..., half_dim:]
    turned = direction * sine_table
    return jnp.concatenate(
        [upper_half * cosine - lower_half * turned, lower_half * cosine + upper_half * turned],
        axis=-1,
    )


def key_mask(query_pos, key_pos, cut_first, cut_last, length):

    def segment(where_at):
        return (where_at >= cut_first).astype(jnp.int32) + (where_at >= cut_last).astype(jnp.int32)

    nearby = jnp.abs(query_pos[:, None] - key_pos[None, :]) <= HALF
    inside = (key_pos >= 0) & (key_pos < length)
    return nearby & inside[None, :] & (segment(query_pos)[:, None] == segment(key_pos)[None, :])


def local(inputs, gain_attn, w_qkv, w_out, gain_mlp, w_in, w_down, bounds, grad_out):
    tokens_dev = inputs.shape[1]
    model_width = inputs.shape[2]
    head_count = model_width // HD
    length = tokens_dev * lax.axis_size("seq")
    offset = lax.axis_index("seq") * tokens_dev
    cut_first = bounds[0, 0]
    cut_last = bounds[0, 1]
    scale_factor = 1.0 / math.sqrt(HD)
    block_rows = math.gcd(tokens_dev, 512)
    key_rows = block_rows + 2 * HALF
    blocks = tokens_dev // block_rows
    gathered = (
        gathered_small(gain_attn, "wshard"),
        lax.all_gather(w_qkv, "wshard", axis=0, tiled=True),
        lax.all_gather(w_out, "wshard", axis=0, tiled=True),
        gathered_small(gain_mlp, "wshard"),
        lax.all_gather(w_in, "wshard", axis=0, tiled=True),
        lax.all_gather(w_down, "wshard", axis=0, tiled=True),
    )
    gain_a = gathered[0].astype(jnp.float32)
    gain_m = gathered[3].astype(jnp.float32)
    stream = inputs[0].astype(jnp.float32)
    normed, norm_back_a = jax.vjp(layer_norm, stream, gain_a)
    normed_low = normed.astype(jnp.bfloat16)
    projected = jnp.dot(normed_low, gathered[1], preferred_element_type=jnp.float32)
    positions = (offset + jnp.arange(tokens_dev, dtype=jnp.int32)).astype(jnp.float32)
    cosine, sine_table = rope_tables(positions, HD)
    query = rotate(
        projected[:, :model_width].reshape(tokens_dev, head_count, HD), cosine, sine_table, 1.0
    ).astype(jnp.bfloat16)
    key_rot = rotate(
        projected[:, model_width : 2 * model_width].reshape(tokens_dev, head_count, HD),
        cosine,
        sine_table,
        1.0,
    )
    key_rot = key_rot.reshape(tokens_dev, model_width).astype(jnp.bfloat16)
    values = projected[:, 2 * model_width :].astype(jnp.bfloat16)
    extended = extended_2(jnp.concatenate([key_rot, values], axis=1), (("seq", 0),), HALF)
    key_ext = extended[:, :model_width].reshape(-1, head_count, HD)
    value_ext = extended[:, model_width:].reshape(-1, head_count, HD)
    query_pos_all = offset + jnp.arange(tokens_dev, dtype=jnp.int32)
    key_pos_all = offset - HALF + jnp.arange(tokens_dev + 2 * HALF, dtype=jnp.int32)

    def block_parts(number):
        rows = number * block_rows
        allowed = key_mask(
            query_pos_all[rows : rows + block_rows],
            key_pos_all[rows : rows + key_rows],
            cut_first,
            cut_last,
            length,
        )
        return (
            query[rows : rows + block_rows],
            key_ext[rows : rows + key_rows],
            value_ext[rows : rows + key_rows],
            allowed,
        )

    def block_scores(query_block, key_block, allowed):
        scores = (
            jnp.einsum("qhd,khd->hqk", query_block, key_block, preferred_element_type=jnp.float32)
            * scale_factor
        )
        return jnp.where(allowed[None], scores, -1e30)

    attended_parts = []
    lse_parts = []
    for number in range(blocks):
        query_block, key_block, value_block, allowed = block_parts(number)
        scores = block_scores(query_block, key_block, allowed)
        top_score = jnp.max(scores, axis=-1, keepdims=True)
        expo = jnp.exp(scores - top_score)
        row_total = jnp.sum(expo, axis=-1, keepdims=True)
        probs = (expo / row_total).astype(jnp.bfloat16)
        attended_parts.append(
            jnp.einsum("hqk,khd->qhd", probs, value_block, preferred_element_type=jnp.float32)
        )
        lse_parts.append(top_score + jnp.log(row_total))
    attended = (
        jnp.concatenate(attended_parts, axis=0)
        .reshape(tokens_dev, model_width)
        .astype(jnp.bfloat16)
    )
    middle = stream + jnp.dot(attended, gathered[2], preferred_element_type=jnp.float32)
    normed2, norm_back_m = jax.vjp(layer_norm, middle, gain_m)
    normed2_low = normed2.astype(jnp.bfloat16)
    lifted = jnp.dot(normed2_low, gathered[4], preferred_element_type=jnp.float32)
    hidden_f, gated_back = jax.vjp(gated_act, lifted)
    hidden = hidden_f.astype(jnp.bfloat16)
    result = middle + jnp.dot(hidden, gathered[5], preferred_element_type=jnp.float32)
    output = result.astype(jnp.bfloat16)[None]
    backward_weights = gathered
    weight_qkv_b = backward_weights[1]
    weight_out_b = backward_weights[2]
    weight_in_b = backward_weights[4]
    weight_down_b = backward_weights[5]
    upstream = grad_out[0].astype(jnp.float32)
    down_grad_low = grad_out[0]
    grad_w_down = jnp.einsum("tf,td->fd", hidden, down_grad_low, preferred_element_type=jnp.float32)
    grad_hidden = jnp.einsum(
        "td,fd->tf", down_grad_low, weight_down_b, preferred_element_type=jnp.float32
    )
    grad_lifted = gated_back(grad_hidden)[0].astype(jnp.bfloat16)
    grad_w_in = jnp.einsum(
        "td,tf->df", normed2_low, grad_lifted, preferred_element_type=jnp.float32
    )
    grad_normed2 = jnp.einsum(
        "tf,df->td", grad_lifted, weight_in_b, preferred_element_type=jnp.float32
    )
    grad_mid_norm, grad_gain_m = norm_back_m(grad_normed2)
    grad_middle = upstream + grad_mid_norm
    branch_grad_low = grad_middle.astype(jnp.bfloat16)
    grad_w_out = jnp.einsum(
        "td,te->de", attended, branch_grad_low, preferred_element_type=jnp.float32
    )
    grad_attended = jnp.einsum(
        "te,de->td", branch_grad_low, weight_out_b, preferred_element_type=jnp.float32
    )
    grad_attended = grad_attended.astype(jnp.bfloat16).reshape(tokens_dev, head_count, HD)
    kv_grad = jnp.zeros((tokens_dev + 2 * HALF, 2 * model_width), jnp.float32)
    query_grads = []
    for number in range(blocks):
        rows = number * block_rows
        query_block, key_block, value_block, allowed = block_parts(number)
        attended_grad_block = grad_attended[rows : rows + block_rows]
        scores = block_scores(query_block, key_block, allowed)
        probs = jnp.exp(scores - lse_parts[number])
        prob_grad = jnp.einsum(
            "qhd,khd->hqk", attended_grad_block, value_block, preferred_element_type=jnp.float32
        )
        centre = jnp.sum(probs * prob_grad, axis=-1, keepdims=True)
        score_grad = (probs * (prob_grad - centre)).astype(jnp.bfloat16)
        query_grads.append(
            jnp.einsum("hqk,khd->qhd", score_grad, key_block, preferred_element_type=jnp.float32)
            * scale_factor
        )
        key_part = (
            jnp.einsum("hqk,qhd->khd", score_grad, query_block, preferred_element_type=jnp.float32)
            * scale_factor
        )
        value_part = jnp.einsum(
            "hqk,qhd->khd",
            probs.astype(jnp.bfloat16),
            attended_grad_block,
            preferred_element_type=jnp.float32,
        )
        joined = jnp.concatenate(
            [key_part.reshape(key_rows, model_width), value_part.reshape(key_rows, model_width)],
            axis=1,
        )
        kv_grad = kv_grad.at[rows : rows + key_rows].add(joined)
    from_next = from_behind(kv_grad[:HALF].astype(jnp.bfloat16), "seq", -1).astype(jnp.float32)
    from_prev = from_behind(kv_grad[tokens_dev + HALF :].astype(jnp.bfloat16), "seq", 1).astype(
        jnp.float32
    )
    own_grad = kv_grad[HALF : HALF + tokens_dev]
    own_grad = own_grad.at[:HALF].add(from_prev)
    own_grad = own_grad.at[tokens_dev - HALF :].add(from_next)
    key_grad_low = own_grad[:, :model_width].astype(jnp.bfloat16)
    value_grad_low = own_grad[:, model_width:].astype(jnp.bfloat16)
    key_raw_grad = rotate(
        key_grad_low.astype(jnp.float32).reshape(tokens_dev, head_count, HD),
        cosine,
        sine_table,
        -1.0,
    )
    key_raw_grad = key_raw_grad.reshape(tokens_dev, model_width).astype(jnp.bfloat16)
    query_grad_low = jnp.concatenate(query_grads, axis=0).astype(jnp.bfloat16)
    query_raw_grad = rotate(query_grad_low.astype(jnp.float32), cosine, sine_table, -1.0)
    query_raw_grad = query_raw_grad.reshape(tokens_dev, model_width).astype(jnp.bfloat16)
    grad_projected = jnp.concatenate([query_raw_grad, key_raw_grad, value_grad_low], axis=1)
    grad_w_qkv = jnp.einsum(
        "td,te->de", normed_low, grad_projected, preferred_element_type=jnp.float32
    )
    grad_normed = jnp.einsum(
        "te,de->td", grad_projected, weight_qkv_b, preferred_element_type=jnp.float32
    )
    grad_stream_norm, grad_gain_a = norm_back_a(grad_normed)
    input_grad = (grad_middle + grad_stream_norm).astype(jnp.bfloat16)[None]
    owners = lax.axis_size("wshard")
    gains = reduced(
        jnp.stack([grad_gain_a.reshape(owners, -1), grad_gain_m.reshape(owners, -1)], axis=1),
        "wshard",
        "seq",
    )
    return (
        output,
        input_grad,
        gains[0],
        total_of(grad_w_qkv),
        total_of(grad_w_out),
        gains[1],
        total_of(grad_w_in),
        total_of(grad_w_down),
    )


def solution(mesh):
    return jax.shard_map(
        local,
        mesh=mesh,
        in_specs=(
            P("wshard", "seq", None),
            P("wshard"),
            P("wshard", None),
            P("wshard", None),
            P("wshard"),
            P("wshard", None),
            P("wshard", None),
            P("wshard", None),
            P("wshard", "seq", None),
        ),
        out_specs=(
            P("wshard", "seq", None),
            P("wshard", "seq", None),
            P("wshard"),
            P("wshard", None),
            P("wshard", None),
            P("wshard"),
            P("wshard", None),
            P("wshard", None),
        ),
        check_vma=False,
    )
```

```python
import math

import jax
import jax.numpy as jnp
from jax import lax
from jax.experimental import pallas as pl
from jax.experimental.pallas import tpu as pltpu
from jax.sharding import PartitionSpec as P

HD = 64
HALF = 64


rope_base = 10000.0


def extended_2(shard, sides, width):
    for axis, dim in sides:
        size, length = (lax.axis_size(axis), shard.shape[dim])
        up = [(i, (i + 1) % size) for i in range(size - 1)]
        down = [(j, i) for i, j in up]
        last = lax.slice_in_dim(shard, length - width, length, axis=dim)
        leading = lax.slice_in_dim(shard, 0, width, axis=dim)
        before = lax.ppermute(last, axis, up)
        after = lax.ppermute(leading, axis, down)
        shard = jnp.concatenate([before, shard, after], axis=dim)
    return shard


def from_behind(shard, axis, by):
    size = lax.axis_size(axis)
    pairs = [(i, i + by) for i in range(size) if 0 <= i + by < size]
    return lax.ppermute(shard, axis, pairs)


def swap(shard, axis, bit):
    return lax.ppermute(shard, axis, [(i, i ^ bit) for i in range(lax.axis_size(axis))])


def bits_of(axis):
    return [1 << b for b in range(lax.axis_size(axis).bit_length() - 1)]


def gathered_small(shard, axis):
    parts = shard[None]
    for bit in bits_of(axis):
        other = swap(parts, axis, bit)
        upper = (lax.axis_index(axis) & bit) > 0
        parts = jnp.concatenate(
            [jnp.where(upper, other, parts), jnp.where(upper, parts, other)], axis=0
        )
    return parts.reshape((-1,) + shard.shape[1:])


def reduced(term, owner_axis, sum_axis):
    for bit in bits_of(owner_axis):
        side = ((lax.axis_index(owner_axis) & bit) > 0).astype(jnp.int32)
        pairs = term.reshape((term.shape[0] // 2, 2) + term.shape[1:])
        kept = lax.dynamic_index_in_dim(pairs, side, 1, keepdims=False)
        sent = lax.dynamic_index_in_dim(pairs, 1 - side, 1, keepdims=False)
        term = kept + swap(sent, owner_axis, bit)
    total = term[0]
    halved = []
    bits = bits_of(sum_axis)
    for bit in bits:
        rows = total.shape[0]
        if bit != bits[-1] and rows % 32 == 0:
            side = ((lax.axis_index(sum_axis) & bit) > 0).astype(jnp.int32)
            kept = lax.dynamic_slice_in_dim(total, side * (rows // 2), rows // 2, 0)
            sent = lax.dynamic_slice_in_dim(total, (1 - side) * (rows // 2), rows // 2, 0)
            total = kept + swap(sent, sum_axis, bit)
            halved.append(bit)
        else:
            total = total + swap(total, sum_axis, bit)
    for bit in reversed(halved):
        other = swap(total, sum_axis, bit)
        upper = (lax.axis_index(sum_axis) & bit) > 0
        total = jnp.concatenate(
            [jnp.where(upper, other, total), jnp.where(upper, total, other)], axis=0
        )
    return total


def total_of(grad):
    owners = lax.axis_size("wshard")
    term = grad.astype(jnp.bfloat16).reshape(owners, grad.shape[0] // owners, grad.shape[1])
    return reduced(term, "wshard", "seq").astype(jnp.float32)


def rope_tables(positions, head_dim):
    frequency = rope_base ** (-(jnp.arange(head_dim // 2, dtype=jnp.float32) * 2.0) / head_dim)
    angles = positions[:, None] * frequency[None, :]
    return (jnp.cos(angles)[:, None, :], jnp.sin(angles)[:, None, :])


ROWS = 256
QROWS = 128
LANES = 128
VMEM = 52 * 1024 * 1024
NT = (((1,), (1,)), ((), ()))
TN = (((0,), (0,)), ((), ()))


def mm(a, b, dims=(((1,), (0,)), ((), ()))):
    return lax.dot_general(a, b, dims, preferred_element_type=jnp.float32)


def standardised(stream):
    centred = stream - jnp.mean(stream, axis=-1, keepdims=True)
    scale = lax.rsqrt(jnp.mean(centred * centred, axis=-1, keepdims=True) + 1e-05)
    return centred * scale, scale


def norm_back(grad, unit, scale, gain):
    scaled = grad * gain
    first = jnp.mean(scaled, axis=-1, keepdims=True)
    second = jnp.mean(scaled * unit, axis=-1, keepdims=True)
    return scale * (scaled - first - unit * second)


def turn(chunk, cosine, sine_low, sine_high):
    ahead = pltpu.roll(chunk, LANES - HD // 2, 1)
    behind = pltpu.roll(chunk, HD // 2, 1)
    return chunk * cosine + ahead * sine_low + behind * sine_high


def qkv_kernel(x_ref, gain_ref, w_ref, cos_ref, low_ref, high_ref, normed_ref, q_ref, kv_ref):
    width = x_ref.shape[1]
    unit, _ = standardised(x_ref[...].astype(jnp.float32))
    normed = (unit * gain_ref[...]).astype(jnp.bfloat16)
    normed_ref[...] = normed
    cosine, low, high = cos_ref[...], low_ref[...], high_ref[...]
    for part in range(3):
        block = mm(normed, w_ref[:, part * width : (part + 1) * width])
        for c in range(0, width, LANES):
            chunk = block[:, c : c + LANES]
            if part < 2:
                chunk = turn(chunk, cosine, low, high)
            chunk = chunk.astype(jnp.bfloat16)
            if part == 0:
                q_ref[:, c : c + LANES] = chunk
            else:
                base = (part - 1) * width + c
                kv_ref[:, base : base + LANES] = chunk


def band_mask(meta_ref):
    start = meta_ref[2] + pl.program_id(0) * QROWS
    shape = (QROWS, QROWS + 2 * HALF)
    row = lax.broadcasted_iota(jnp.int32, shape, 0)
    col = lax.broadcasted_iota(jnp.int32, shape, 1)
    query_pos = start + row
    key_pos = start - HALF + col
    cut_first, cut_last = meta_ref[0], meta_ref[1]

    def segment(at):
        return (at >= cut_first).astype(jnp.int32) + (at >= cut_last).astype(jnp.int32)

    near = jnp.abs(query_pos - key_pos) <= HALF
    inside = (key_pos >= 0) & (key_pos < meta_ref[3])
    return near & inside & (segment(query_pos) == segment(key_pos))


def lower_lanes(rows):
    return lax.broadcasted_iota(jnp.int32, (rows, LANES), 1) < HD


def attend_kernel(meta_ref, q_ref, kv_ref, out_ref, lse_ref):
    width = q_ref.shape[1]
    allowed = band_mask(meta_ref)
    lower = lower_lanes(QROWS)
    rows = pl.ds(pl.multiple_of(pl.program_id(0) * QROWS, QROWS), QROWS + 2 * HALF)
    scale = 1.0 / math.sqrt(HD)
    lane = lax.broadcasted_iota(jnp.int32, (QROWS, LANES), 1)
    lses = jnp.zeros((QROWS, LANES), jnp.float32)
    for c in range(0, width, LANES):
        q = q_ref[:, c : c + LANES]
        k = kv_ref[rows, c : c + LANES]
        v = kv_ref[rows, width + c : width + c + LANES]
        outs = []
        for half in range(2):
            mine = lower if half == 0 else jnp.logical_not(lower)
            scores = mm(jnp.where(mine, q, jnp.zeros_like(q)), k, NT) * scale
            scores = jnp.where(allowed, scores, -1e30)
            top = jnp.max(scores, axis=-1, keepdims=True)
            expo = jnp.exp(scores - top)
            total = jnp.sum(expo, axis=-1, keepdims=True)
            probs = (expo * (1.0 / total)).astype(jnp.bfloat16)
            outs.append(mm(probs, v))
            lses = jnp.where(lane == c // HD + half, top + jnp.log(total), lses)
        out_ref[:, c : c + LANES] = jnp.where(lower, outs[0], outs[1]).astype(jnp.bfloat16)
    lse_ref[...] = lses


def attend_back_kernel(
    meta_ref, q_ref, go_ref, kv_ref, lse_ref, cos_ref, low_ref, high_ref, dq_ref, dkv_ref
):
    width = q_ref.shape[1]

    @pl.when(pl.program_id(0) == 0)
    def _():
        dkv_ref[...] = jnp.zeros_like(dkv_ref)

    allowed = band_mask(meta_ref)
    lower = lower_lanes(QROWS)
    rows = pl.ds(pl.multiple_of(pl.program_id(0) * QROWS, QROWS), QROWS + 2 * HALF)
    scale = 1.0 / math.sqrt(HD)
    for c in range(0, width, LANES):
        q = q_ref[:, c : c + LANES]
        go = go_ref[:, c : c + LANES]
        k = kv_ref[rows, c : c + LANES]
        v = kv_ref[rows, width + c : width + c + LANES]
        dqs = []
        dk = dv = None
        for half in range(2):
            mine = lower if half == 0 else jnp.logical_not(lower)
            q_half = jnp.where(mine, q, jnp.zeros_like(q))
            go_half = jnp.where(mine, go, jnp.zeros_like(go))
            head = c // HD + half
            scores = mm(q_half, k, NT) * scale
            scores = jnp.where(allowed, scores, -1e30)
            probs = jnp.exp(scores - lse_ref[:, head : head + 1])
            prob_grad = mm(go_half, v, NT)
            centre = jnp.sum(probs * prob_grad, axis=-1, keepdims=True)
            score_grad = (probs * (prob_grad - centre)).astype(jnp.bfloat16)
            dqs.append(mm(score_grad, k))
            dk_half = mm(score_grad, q_half, TN)
            dv_half = mm(probs.astype(jnp.bfloat16), go_half, TN)
            dk = dk_half if dk is None else dk + dk_half
            dv = dv_half if dv is None else dv + dv_half
        dq = (jnp.where(lower, dqs[0], dqs[1]) * scale).astype(jnp.bfloat16).astype(jnp.float32)
        dq_ref[:, c : c + LANES] = turn(
            dq, cos_ref[...], -low_ref[...], -high_ref[...]
        ).astype(jnp.bfloat16)
        dkv_ref[rows, c : c + LANES] += dk * scale
        dkv_ref[rows, width + c : width + c + LANES] += dv


def mlp_kernel(
    x_ref, att_ref, g_ref, gain_ref, wo_ref, wi_ref, wd_ref,
    out_ref, normed_ref, hidden_ref, gl_ref, gmid_ref, gm_ref, gatt_ref, ggain_ref,
):
    wide = wd_ref.shape[0]
    middle = x_ref[...].astype(jnp.float32) + mm(att_ref[...], wo_ref[...])
    unit, spread = standardised(middle)
    gain = gain_ref[...]
    normed = (unit * gain).astype(jnp.bfloat16)
    normed_ref[...] = normed
    active = mm(normed, wi_ref[:, :wide])
    gate = mm(normed, wi_ref[:, wide:])
    cdf = 0.5 * (1.0 + lax.erf(active * math.sqrt(0.5)))
    act = active * cdf
    hidden = (act * gate).astype(jnp.bfloat16)
    hidden_ref[...] = hidden
    out_ref[...] = (middle + mm(hidden, wd_ref[...])).astype(jnp.bfloat16)
    gd = g_ref[...]
    grad_hidden = mm(gd, wd_ref[...], NT)
    slope = cdf + active * (jnp.exp(-0.5 * active * active) * (1.0 / math.sqrt(2.0 * math.pi)))
    grad_active = (grad_hidden * gate * slope).astype(jnp.bfloat16)
    grad_gate = (grad_hidden * act).astype(jnp.bfloat16)
    gl_ref[:, :wide] = grad_active
    gl_ref[:, wide:] = grad_gate
    grad_normed = mm(grad_active, wi_ref[:, :wide], NT) + mm(grad_gate, wi_ref[:, wide:], NT)

    @pl.when(pl.program_id(0) == 0)
    def _():
        ggain_ref[...] = jnp.zeros_like(ggain_ref)

    ggain_ref[...] += jnp.sum(grad_normed * unit, axis=0, keepdims=True)
    grad_middle = gd.astype(jnp.float32) + norm_back(grad_normed, unit, spread, gain)
    gmid_ref[...] = grad_middle
    gm = grad_middle.astype(jnp.bfloat16)
    gm_ref[...] = gm
    gatt_ref[...] = mm(gm, wo_ref[...], NT).astype(jnp.bfloat16)


def last_kernel(
    x_ref, gain_ref, w_ref, dq_ref, dkv_ref, prev_ref, next_ref, cos_ref, low_ref, high_ref,
    gmid_ref, gp_ref, out_ref, ggain_ref,
):
    width = x_ref.shape[1]
    step = pl.program_id(0)
    start = pl.multiple_of(step * ROWS + HALF, HALF)
    first = (step == 0).astype(jnp.float32)
    last = (step == pl.num_programs(0) - 1).astype(jnp.float32)
    gp_ref[:, :width] = dq_ref[...]
    for c in range(0, 2 * width, LANES):
        own = dkv_ref[pl.ds(start, ROWS), c : c + LANES]
        top = own[:HALF] + prev_ref[:, c : c + LANES].astype(jnp.float32) * first
        low_end = own[ROWS - HALF :] + next_ref[:, c : c + LANES].astype(jnp.float32) * last
        chunk = jnp.concatenate([top, own[HALF : ROWS - HALF], low_end], axis=0)
        chunk = chunk.astype(jnp.bfloat16)
        if c < width:
            chunk = turn(
                chunk.astype(jnp.float32), cos_ref[...], -low_ref[...], -high_ref[...]
            ).astype(jnp.bfloat16)
        gp_ref[:, width + c : width + c + LANES] = chunk
    grad_normed = mm(gp_ref[...], w_ref[...], NT)
    unit, spread = standardised(x_ref[...].astype(jnp.float32))

    @pl.when(step == 0)
    def _():
        ggain_ref[...] = jnp.zeros_like(ggain_ref)

    ggain_ref[...] += jnp.sum(grad_normed * unit, axis=0, keepdims=True)
    out_ref[...] = (gmid_ref[...] + norm_back(grad_normed, unit, spread, gain_ref[...])).astype(
        jnp.bfloat16
    )


def run(body, steps, ins, outs, flops):
    def spec(array, rows):
        if rows == 0:
            return pl.BlockSpec(memory_space=pltpu.SMEM)
        if rows is None:
            return pl.BlockSpec(array.shape, lambda i: (0, 0))
        return pl.BlockSpec((rows, array.shape[1]), lambda i: (i, 0))

    moved = sum(a.size * a.dtype.itemsize for a, _ in ins + outs)
    return pl.pallas_call(
        body,
        grid=(steps,),
        in_specs=[spec(a, r) for a, r in ins],
        out_specs=[spec(a, r) for a, r in outs],
        out_shape=[a for a, _ in outs],
        compiler_params=pltpu.CompilerParams(
            vmem_limit_bytes=VMEM, dimension_semantics=("arbitrary",)
        ),
        cost_estimate=pl.CostEstimate(
            flops=int(flops), bytes_accessed=int(moved), transcendentals=0
        ),
    )(*[a for a, _ in ins])


def local(inputs, gain_attn, w_qkv, w_out, gain_mlp, w_in, w_down, bounds, grad_out):
    tokens = inputs.shape[1]
    width = inputs.shape[2]
    length = tokens * lax.axis_size("seq")
    offset = lax.axis_index("seq") * tokens
    shape = jax.ShapeDtypeStruct
    bf16, f32 = jnp.bfloat16, jnp.float32
    gains_all = gathered_small(jnp.stack([gain_attn, gain_mlp], axis=1), "wshard")
    gain_a = gains_all[:, 0].astype(f32)[None]
    gain_m = gains_all[:, 1].astype(f32)[None]
    weight_qkv = lax.all_gather(w_qkv, "wshard", axis=0, tiled=True)
    weight_out = lax.all_gather(w_out, "wshard", axis=0, tiled=True)
    weight_in = lax.all_gather(w_in, "wshard", axis=0, tiled=True)
    weight_down = lax.all_gather(w_down, "wshard", axis=0, tiled=True)
    wide = weight_down.shape[0]
    stream = inputs[0]
    upstream = grad_out[0]
    positions = (offset + jnp.arange(tokens, dtype=jnp.int32)).astype(f32)
    cosine, sine = rope_tables(positions, HD)
    cosine, sine = cosine[:, 0], sine[:, 0]
    none = jnp.zeros_like(sine)
    cos_t = jnp.concatenate([cosine] * 4, axis=1)
    low_t = jnp.concatenate([-sine, none] * 2, axis=1)
    high_t = jnp.concatenate([none, sine] * 2, axis=1)
    steps, qsteps = tokens // ROWS, tokens // QROWS
    normed, query, kv = run(
        qkv_kernel,
        steps,
        [(stream, ROWS), (gain_a, None), (weight_qkv, None)]
        + [(cos_t, ROWS), (low_t, ROWS), (high_t, ROWS)],
        [
            (shape((tokens, width), bf16), ROWS),
            (shape((tokens, width), bf16), ROWS),
            (shape((tokens, 2 * width), bf16), ROWS),
        ],
        6 * tokens * width * width,
    )
    kv_ext = extended_2(kv, (("seq", 0),), HALF)
    meta = jnp.stack([bounds[0, 0], bounds[0, 1], offset, jnp.int32(length)]).astype(jnp.int32)
    attended, lse = run(
        attend_kernel,
        qsteps,
        [(meta, 0), (query, QROWS), (kv_ext, None)],
        [(shape((tokens, width), bf16), QROWS), (shape((tokens, LANES), f32), QROWS)],
        16 * tokens * width * QROWS,
    )
    output, normed2, hidden, grad_lifted, grad_middle, grad_mid_low, grad_att, grad_gain_m = run(
        mlp_kernel,
        steps,
        [(stream, ROWS), (attended, ROWS), (upstream, ROWS), (gain_m, None)]
        + [(weight_out, None), (weight_in, None), (weight_down, None)],
        [
            (shape((tokens, width), bf16), ROWS),
            (shape((tokens, width), bf16), ROWS),
            (shape((tokens, wide), bf16), ROWS),
            (shape((tokens, 2 * wide), bf16), ROWS),
            (shape((tokens, width), f32), ROWS),
            (shape((tokens, width), bf16), ROWS),
            (shape((tokens, width), bf16), ROWS),
            (shape((1, width), f32), None),
        ],
        4 * tokens * width * (width + 3 * wide),
    )
    grad_w_down = mm(hidden, upstream, TN)
    grad_w_in = mm(normed2, grad_lifted, TN)
    grad_w_out = mm(attended, grad_mid_low, TN)
    query_grad, kv_grad = run(
        attend_back_kernel,
        qsteps,
        [(meta, 0), (query, QROWS), (grad_att, QROWS), (kv_ext, None), (lse, QROWS)]
        + [(cos_t, QROWS), (low_t, QROWS), (high_t, QROWS)],
        [
            (shape((tokens, width), bf16), QROWS),
            (shape((tokens + 2 * HALF, 2 * width), f32), None),
        ],
        40 * tokens * width * QROWS,
    )
    from_next = from_behind(kv_grad[:HALF].astype(bf16), "seq", -1)
    from_prev = from_behind(kv_grad[tokens + HALF :].astype(bf16), "seq", 1)
    grad_projected, input_grad, grad_gain_a = run(
        last_kernel,
        steps,
        [(stream, ROWS), (gain_a, None), (weight_qkv, None), (query_grad, ROWS), (kv_grad, None)]
        + [(from_prev, None), (from_next, None)]
        + [(cos_t, ROWS), (low_t, ROWS), (high_t, ROWS), (grad_middle, ROWS)],
        [
            (shape((tokens, 3 * width), bf16), ROWS),
            (shape((tokens, width), bf16), ROWS),
            (shape((1, width), f32), None),
        ],
        6 * tokens * width * width,
    )
    grad_w_qkv = mm(normed, grad_projected, TN)
    output, input_grad = output[None], input_grad[None]
    owners = lax.axis_size("wshard")
    gains = reduced(
        jnp.stack([grad_gain_a.reshape(owners, -1), grad_gain_m.reshape(owners, -1)], axis=1),
        "wshard",
        "seq",
    )
    return (
        output,
        input_grad,
        gains[0],
        total_of(grad_w_qkv),
        total_of(grad_w_out),
        gains[1],
        total_of(grad_w_in),
        total_of(grad_w_down),
    )


def solution(mesh):
    return jax.shard_map(
        local,
        mesh=mesh,
        in_specs=(
            P("wshard", "seq", None),
            P("wshard"),
            P("wshard", None),
            P("wshard", None),
            P("wshard"),
            P("wshard", None),
            P("wshard", None),
            P("wshard", None),
            P("wshard", "seq", None),
        ),
        out_specs=(
            P("wshard", "seq", None),
            P("wshard", "seq", None),
            P("wshard"),
            P("wshard", None),
            P("wshard", None),
            P("wshard"),
            P("wshard", None),
            P("wshard", None),
        ),
        check_vma=False,
    )
```

```python
import functools
import math

import jax
import jax.numpy as jnp
from jax import lax
from jax.experimental import pallas as pl
from jax.experimental.pallas import tpu as pltpu
from jax.sharding import PartitionSpec as P

HD = 64
HALF = 64


rope_base = 10000.0


def extended_2(shard, sides, width):
    for axis, dim in sides:
        size, length = (lax.axis_size(axis), shard.shape[dim])
        up = [(i, (i + 1) % size) for i in range(size - 1)]
        down = [(j, i) for i, j in up]
        last = lax.slice_in_dim(shard, length - width, length, axis=dim)
        leading = lax.slice_in_dim(shard, 0, width, axis=dim)
        before = lax.ppermute(last, axis, up)
        after = lax.ppermute(leading, axis, down)
        shard = jnp.concatenate([before, shard, after], axis=dim)
    return shard


def from_behind(shard, axis, by):
    size = lax.axis_size(axis)
    pairs = [(i, i + by) for i in range(size) if 0 <= i + by < size]
    return lax.ppermute(shard, axis, pairs)


def swap(shard, axis, bit):
    return lax.ppermute(shard, axis, [(i, i ^ bit) for i in range(lax.axis_size(axis))])


def bits_of(axis):
    return [1 << b for b in range(lax.axis_size(axis).bit_length() - 1)]


def gathered_by_swaps(shard, axis):
    size, me = lax.axis_size(axis), lax.axis_index(axis)
    parts = shard[None]
    for bit in reversed(bits_of(axis)):
        other = swap(parts, axis, bit)
        upper = (me & bit) > 0
        parts = jnp.stack(
            [jnp.where(upper, other, parts), jnp.where(upper, parts, other)], axis=1
        ).reshape((-1,) + shard.shape)
    return parts.reshape((size * shard.shape[0],) + shard.shape[1:])


def owner_step(term, axis, bit):
    side = ((lax.axis_index(axis) & bit) > 0).astype(jnp.int32)
    pairs = term.reshape((term.shape[0] // 2, 2) + term.shape[1:])
    kept = lax.dynamic_index_in_dim(pairs, side, 1, keepdims=False)
    sent = lax.dynamic_index_in_dim(pairs, 1 - side, 1, keepdims=False)
    return kept + swap(sent, axis, bit)


def sum_step(total, axis, bit, halved):
    rows = total.shape[0]
    if bit == bits_of(axis)[-1] or rows % 32:
        return total + swap(total, axis, bit), halved
    side = ((lax.axis_index(axis) & bit) > 0).astype(jnp.int32)
    kept = lax.dynamic_slice_in_dim(total, side * (rows // 2), rows // 2, 0)
    sent = lax.dynamic_slice_in_dim(total, (1 - side) * (rows // 2), rows // 2, 0)
    return kept + swap(sent, axis, bit), halved + [bit]


def summed(total, axis, done=0, halved=()):
    halved = list(halved)
    for bit in bits_of(axis)[done:]:
        total, halved = sum_step(total, axis, bit, halved)
    for bit in reversed(halved):
        other = swap(total, axis, bit)
        upper = (lax.axis_index(axis) & bit) > 0
        total = jnp.concatenate(
            [jnp.where(upper, other, total), jnp.where(upper, total, other)], axis=0
        )
    return total


def reduced(term, owner_axis, sum_axis):
    while term.shape[0] > 1:
        bit = lax.axis_size(owner_axis) // term.shape[0]
        term = owner_step(term, owner_axis, bit)
    return summed(term[0], sum_axis)


def term_of(grad):
    owners = lax.axis_size("wshard")
    return grad.astype(jnp.bfloat16).reshape(owners, grad.shape[0] // owners, grad.shape[1])


def total_of(term):
    return reduced(term, "wshard", "seq").astype(jnp.float32)


def rope_tables(positions, head_dim):
    frequency = rope_base ** (-(jnp.arange(head_dim // 2, dtype=jnp.float32) * 2.0) / head_dim)
    angles = positions[:, None] * frequency[None, :]
    return (jnp.cos(angles)[:, None, :], jnp.sin(angles)[:, None, :])


ROWS = 256
QROWS = 128
LANES = 128
VMEM = 52 * 1024 * 1024
NT = (((1,), (1,)), ((), ()))
TN = (((0,), (0,)), ((), ()))


def mm(a, b, dims=(((1,), (0,)), ((), ()))):
    return lax.dot_general(a, b, dims, preferred_element_type=jnp.float32)


def standardised(stream):
    centred = stream - jnp.mean(stream, axis=-1, keepdims=True)
    scale = lax.rsqrt(jnp.mean(centred * centred, axis=-1, keepdims=True) + 1e-05)
    return centred * scale, scale


def norm_back(grad, unit, scale, gain):
    scaled = grad * gain
    first = jnp.mean(scaled, axis=-1, keepdims=True)
    second = jnp.mean(scaled * unit, axis=-1, keepdims=True)
    return scale * (scaled - first - unit * second)


def turn(chunk, cosine, sine_low, sine_high):
    ahead = pltpu.roll(chunk, LANES - HD // 2, 1)
    behind = pltpu.roll(chunk, HD // 2, 1)
    return chunk * cosine + ahead * sine_low + behind * sine_high


def qkv_kernel(x_ref, gain_ref, w_ref, cos_ref, low_ref, high_ref, normed_ref, q_ref, kv_ref):
    width = x_ref.shape[1]
    unit, _ = standardised(x_ref[...].astype(jnp.float32))
    normed = (unit * gain_ref[...]).astype(jnp.bfloat16)
    normed_ref[...] = normed
    cosine, low, high = cos_ref[...], low_ref[...], high_ref[...]
    for part in range(3):
        block = mm(normed, w_ref[:, part * width : (part + 1) * width])
        for c in range(0, width, LANES):
            chunk = block[:, c : c + LANES]
            if part < 2:
                chunk = turn(chunk, cosine, low, high)
            chunk = chunk.astype(jnp.bfloat16)
            if part == 0:
                q_ref[:, c : c + LANES] = chunk
            else:
                base = (part - 1) * width + c
                kv_ref[:, base : base + LANES] = chunk


def band_mask(meta_ref):
    start = meta_ref[2] + pl.program_id(0) * QROWS
    shape = (QROWS, QROWS + 2 * HALF)
    row = lax.broadcasted_iota(jnp.int32, shape, 0)
    col = lax.broadcasted_iota(jnp.int32, shape, 1)
    query_pos = start + row
    key_pos = start - HALF + col
    cut_first, cut_last = meta_ref[0], meta_ref[1]

    def segment(at):
        return (at >= cut_first).astype(jnp.int32) + (at >= cut_last).astype(jnp.int32)

    near = jnp.abs(query_pos - key_pos) <= HALF
    inside = (key_pos >= 0) & (key_pos < meta_ref[3])
    return near & inside & (segment(query_pos) == segment(key_pos))


def lower_lanes(rows):
    return lax.broadcasted_iota(jnp.int32, (rows, LANES), 1) < HD


def attend_kernel(meta_ref, q_ref, kv_ref, out_ref, lse_ref):
    width = q_ref.shape[1]
    allowed = band_mask(meta_ref)
    lower = lower_lanes(QROWS)
    rows = pl.ds(pl.multiple_of(pl.program_id(0) * QROWS, QROWS), QROWS + 2 * HALF)
    scale = 1.0 / math.sqrt(HD)
    lane = lax.broadcasted_iota(jnp.int32, (QROWS, LANES), 1)
    lses = jnp.zeros((QROWS, LANES), jnp.float32)
    for c in range(0, width, LANES):
        q = q_ref[:, c : c + LANES]
        k = kv_ref[rows, c : c + LANES]
        v = kv_ref[rows, width + c : width + c + LANES]
        outs = []
        for half in range(2):
            mine = lower if half == 0 else jnp.logical_not(lower)
            scores = mm(jnp.where(mine, q, jnp.zeros_like(q)), k, NT) * scale
            scores = jnp.where(allowed, scores, -1e30)
            top = jnp.max(scores, axis=-1, keepdims=True)
            expo = jnp.exp(scores - top)
            total = jnp.sum(expo, axis=-1, keepdims=True)
            probs = (expo * (1.0 / total)).astype(jnp.bfloat16)
            outs.append(mm(probs, v))
            lses = jnp.where(lane == c // HD + half, top + jnp.log(total), lses)
        out_ref[:, c : c + LANES] = jnp.where(lower, outs[0], outs[1]).astype(jnp.bfloat16)
    lse_ref[...] = lses


def attend_back_kernel(
    group, meta_ref, q_ref, go_ref, k_ref, v_ref, lse_ref, cos_ref, low_ref, high_ref,
    dq_ref, dk_ref, dv_ref,
):
    width = q_ref.shape[1]

    @pl.when(pl.program_id(0) == 0)
    def _():
        dk_ref[...] = jnp.zeros_like(dk_ref)
        dv_ref[...] = jnp.zeros_like(dv_ref)

    allowed = band_mask(meta_ref)
    lower = lower_lanes(QROWS)
    rows = pl.ds(pl.multiple_of(pl.program_id(0) * QROWS, QROWS), QROWS + 2 * HALF)
    scale = 1.0 / math.sqrt(HD)
    for c in range(0, width, LANES):
        q = q_ref[:, c : c + LANES]
        go = go_ref[:, c : c + LANES]
        k = k_ref[rows, c : c + LANES]
        v = v_ref[rows, c : c + LANES]
        dqs = []
        dk = dv = None
        for half in range(2):
            mine = lower if half == 0 else jnp.logical_not(lower)
            q_half = jnp.where(mine, q, jnp.zeros_like(q))
            go_half = jnp.where(mine, go, jnp.zeros_like(go))
            head = (group * width + c) // HD + half
            scores = mm(q_half, k, NT) * scale
            scores = jnp.where(allowed, scores, -1e30)
            probs = jnp.exp(scores - lse_ref[:, head : head + 1])
            prob_grad = mm(go_half, v, NT)
            centre = jnp.sum(probs * prob_grad, axis=-1, keepdims=True)
            score_grad = (probs * (prob_grad - centre)).astype(jnp.bfloat16)
            dqs.append(mm(score_grad, k))
            dk_half = mm(score_grad, q_half, TN)
            dv_half = mm(probs.astype(jnp.bfloat16), go_half, TN)
            dk = dk_half if dk is None else dk + dk_half
            dv = dv_half if dv is None else dv + dv_half
        dq = (jnp.where(lower, dqs[0], dqs[1]) * scale).astype(jnp.bfloat16).astype(jnp.float32)
        dq_ref[:, c : c + LANES] = turn(
            dq, cos_ref[...], -low_ref[...], -high_ref[...]
        ).astype(jnp.bfloat16)
        dk_ref[rows, c : c + LANES] += dk * scale
        dv_ref[rows, c : c + LANES] += dv


def mlp_kernel(
    x_ref, att_ref, g_ref, gain_ref, wo_ref, wi_ref, wd_ref,
    out_ref, normed_ref, hidden_ref, gl_ref, gmid_ref, gm_ref, gatt_ref, ggain_ref,
):
    wide = wd_ref.shape[0]
    middle = x_ref[...].astype(jnp.float32) + mm(att_ref[...], wo_ref[...])
    unit, spread = standardised(middle)
    gain = gain_ref[...]
    normed = (unit * gain).astype(jnp.bfloat16)
    normed_ref[...] = normed
    active = mm(normed, wi_ref[:, :wide])
    gate = mm(normed, wi_ref[:, wide:])
    cdf = 0.5 * (1.0 + lax.erf(active * math.sqrt(0.5)))
    act = active * cdf
    hidden = (act * gate).astype(jnp.bfloat16)
    hidden_ref[...] = hidden
    out_ref[...] = (middle + mm(hidden, wd_ref[...])).astype(jnp.bfloat16)
    gd = g_ref[...]
    grad_hidden = mm(gd, wd_ref[...], NT)
    slope = cdf + active * (jnp.exp(-0.5 * active * active) * (1.0 / math.sqrt(2.0 * math.pi)))
    grad_active = (grad_hidden * gate * slope).astype(jnp.bfloat16)
    grad_gate = (grad_hidden * act).astype(jnp.bfloat16)
    gl_ref[:, :wide] = grad_active
    gl_ref[:, wide:] = grad_gate
    grad_normed = mm(grad_active, wi_ref[:, :wide], NT) + mm(grad_gate, wi_ref[:, wide:], NT)

    @pl.when(pl.program_id(0) == 0)
    def _():
        ggain_ref[...] = jnp.zeros_like(ggain_ref)

    ggain_ref[...] += jnp.sum(grad_normed * unit, axis=0, keepdims=True)
    grad_middle = gd.astype(jnp.float32) + norm_back(grad_normed, unit, spread, gain)
    gmid_ref[...] = grad_middle
    gm = grad_middle.astype(jnp.bfloat16)
    gm_ref[...] = gm
    gatt_ref[...] = mm(gm, wo_ref[...], NT).astype(jnp.bfloat16)


def last_kernel(
    x_ref, gain_ref, w_ref, dq0_ref, dq1_ref, dk0_ref, dk1_ref, dv0_ref, dv1_ref, prev_ref,
    next_ref, cos_ref, low_ref, high_ref, gmid_ref, gp_ref, out_ref, ggain_ref,
):
    width = x_ref.shape[1]
    step = pl.program_id(0)
    start = pl.multiple_of(step * ROWS + HALF, HALF)
    first = (step == 0).astype(jnp.float32)
    last = (step == pl.num_programs(0) - 1).astype(jnp.float32)
    part = width // 2
    gp_ref[:, :part] = dq0_ref[...]
    gp_ref[:, part:width] = dq1_ref[...]
    pieces = (dk0_ref, dk1_ref, dv0_ref, dv1_ref)
    for c in range(0, 2 * width, LANES):
        own = pieces[c // part][pl.ds(start, ROWS), c % part : c % part + LANES]
        top = own[:HALF] + prev_ref[:, c : c + LANES].astype(jnp.float32) * first
        low_end = own[ROWS - HALF :] + next_ref[:, c : c + LANES].astype(jnp.float32) * last
        chunk = jnp.concatenate([top, own[HALF : ROWS - HALF], low_end], axis=0)
        chunk = chunk.astype(jnp.bfloat16)
        if c < width:
            chunk = turn(
                chunk.astype(jnp.float32), cos_ref[...], -low_ref[...], -high_ref[...]
            ).astype(jnp.bfloat16)
        gp_ref[:, width + c : width + c + LANES] = chunk
    grad_normed = mm(gp_ref[...], w_ref[...], NT)
    unit, spread = standardised(x_ref[...].astype(jnp.float32))

    @pl.when(step == 0)
    def _():
        ggain_ref[...] = jnp.zeros_like(ggain_ref)

    ggain_ref[...] += jnp.sum(grad_normed * unit, axis=0, keepdims=True)
    out_ref[...] = (gmid_ref[...] + norm_back(grad_normed, unit, spread, gain_ref[...])).astype(
        jnp.bfloat16
    )


def run(body, steps, ins, outs, flops):
    def spec(array, rows):
        if isinstance(rows, tuple):
            rows, cols, place = rows
            if rows is None:
                return pl.BlockSpec((array.shape[0], cols), lambda i: (0, place))
            return pl.BlockSpec((rows, cols), lambda i: (i, place))
        if rows == 0:
            return pl.BlockSpec(memory_space=pltpu.SMEM)
        if rows is None:
            return pl.BlockSpec(array.shape, lambda i: (0, 0))
        return pl.BlockSpec((rows, array.shape[1]), lambda i: (i, 0))

    moved = sum(a.size * a.dtype.itemsize for a, _ in ins + outs)
    return pl.pallas_call(
        body,
        grid=(steps,),
        in_specs=[spec(a, r) for a, r in ins],
        out_specs=[spec(a, r) for a, r in outs],
        out_shape=[a for a, _ in outs],
        compiler_params=pltpu.CompilerParams(
            vmem_limit_bytes=VMEM, dimension_semantics=("arbitrary",)
        ),
        cost_estimate=pl.CostEstimate(
            flops=int(flops), bytes_accessed=int(moved), transcendentals=0
        ),
    )(*[a for a, _ in ins])


def local(inputs, gain_attn, w_qkv, w_out, gain_mlp, w_in, w_down, bounds, grad_out):
    tokens = inputs.shape[1]
    width = inputs.shape[2]
    length = tokens * lax.axis_size("seq")
    offset = lax.axis_index("seq") * tokens
    shape = jax.ShapeDtypeStruct
    bf16, f32 = jnp.bfloat16, jnp.float32
    gains_all = gathered_by_swaps(jnp.stack([gain_attn, gain_mlp], axis=1), "wshard")
    gain_a = gains_all[:, 0].astype(f32)[None]
    gain_m = gains_all[:, 1].astype(f32)[None]
    weight_qkv = lax.all_gather(w_qkv, "wshard", axis=0, tiled=True)
    weight_out = lax.all_gather(w_out, "wshard", axis=0, tiled=True)
    weight_qkv, w_in = lax.optimization_barrier((weight_qkv, w_in))
    weight_in = gathered_by_swaps(w_in, "wshard")
    weight_down = lax.all_gather(w_down, "wshard", axis=0, tiled=True)
    wide = weight_down.shape[0]
    stream = inputs[0]
    upstream = grad_out[0]
    positions = (offset + jnp.arange(tokens, dtype=jnp.int32)).astype(f32)
    cosine, sine = rope_tables(positions, HD)
    cosine, sine = cosine[:, 0], sine[:, 0]
    none = jnp.zeros_like(sine)
    cos_t = jnp.concatenate([cosine] * 4, axis=1)
    low_t = jnp.concatenate([-sine, none] * 2, axis=1)
    high_t = jnp.concatenate([none, sine] * 2, axis=1)
    steps, qsteps = tokens // ROWS, tokens // QROWS
    normed, query, kv = run(
        qkv_kernel,
        steps,
        [(stream, ROWS), (gain_a, None), (weight_qkv, None)]
        + [(cos_t, ROWS), (low_t, ROWS), (high_t, ROWS)],
        [
            (shape((tokens, width), bf16), ROWS),
            (shape((tokens, width), bf16), ROWS),
            (shape((tokens, 2 * width), bf16), ROWS),
        ],
        18 * tokens * width * width,
    )
    kv_ext = extended_2(kv, (("seq", 0),), HALF)
    meta = jnp.stack([bounds[0, 0], bounds[0, 1], offset, jnp.int32(length)]).astype(jnp.int32)
    attended, lse = run(
        attend_kernel,
        qsteps,
        [(meta, 0), (query, QROWS), (kv_ext, None)],
        [(shape((tokens, width), bf16), QROWS), (shape((tokens, LANES), f32), QROWS)],
        150 * tokens * width * QROWS,
    )
    output, normed2, hidden, grad_lifted, grad_middle, grad_mid_low, grad_att, grad_gain_m = run(
        mlp_kernel,
        steps,
        [(stream, ROWS), (attended, ROWS), (upstream, ROWS), (gain_m, None)]
        + [(weight_out, None), (weight_in, None), (weight_down, None)],
        [
            (shape((tokens, width), bf16), ROWS),
            (shape((tokens, width), bf16), ROWS),
            (shape((tokens, wide), bf16), ROWS),
            (shape((tokens, 2 * wide), bf16), ROWS),
            (shape((tokens, width), f32), ROWS),
            (shape((tokens, width), bf16), ROWS),
            (shape((tokens, width), bf16), ROWS),
            (shape((1, width), f32), None),
        ],
        4 * tokens * width * (width + 3 * wide),
    )
    terms = [
        term_of(mm(normed2, grad_lifted, TN)),
        term_of(mm(hidden, upstream, TN)),
        term_of(mm(attended, grad_mid_low, TN)),
    ]
    grad_att, *terms = lax.optimization_barrier((grad_att, *terms))
    part = width // 2
    query_grads, key_grads, value_grads = [], [], []
    for group in range(2):
        dq, dk, dv = run(
            functools.partial(attend_back_kernel, group),
            qsteps,
            [(meta, 0), (query, (QROWS, part, group)), (grad_att, (QROWS, part, group))]
            + [(kv_ext, (None, part, group)), (kv_ext, (None, part, 2 + group)), (lse, QROWS)]
            + [(cos_t, QROWS), (low_t, QROWS), (high_t, QROWS)],
            [(shape((tokens, part), bf16), QROWS)]
            + [(shape((tokens + 2 * HALF, part), f32), None)] * 2,
            200 * tokens * width * QROWS,
        )
        query_grads.append(dq)
        key_grads.append(dk)
        value_grads.append(dv)
        if group == 0:
            terms = [owner_step(term, "wshard", 1) for term in terms]
            dq, grad_att, *terms = lax.optimization_barrier((dq, grad_att, *terms))
            query_grads[0] = dq
    pieces = key_grads + value_grads
    from_next = from_behind(
        jnp.concatenate([piece[:HALF] for piece in pieces], axis=1).astype(bf16), "seq", -1
    )
    from_prev = from_behind(
        jnp.concatenate([piece[tokens + HALF :] for piece in pieces], axis=1).astype(bf16), "seq", 1
    )
    terms = [owner_step(term, "wshard", 2)[0] for term in terms]
    from_next, from_prev, *terms = lax.optimization_barrier((from_next, from_prev, *terms))
    begun = [sum_step(term, "seq", 1, []) for term in terms]
    grad_projected, input_grad, grad_gain_a = run(
        last_kernel,
        steps,
        [(stream, ROWS), (gain_a, None), (weight_qkv, None), (query_grads[0], ROWS)]
        + [(query_grads[1], ROWS)]
        + [(piece, None) for piece in pieces]
        + [(from_prev, None), (from_next, None)]
        + [(cos_t, ROWS), (low_t, ROWS), (high_t, ROWS), (grad_middle, ROWS)],
        [
            (shape((tokens, 3 * width), bf16), ROWS),
            (shape((tokens, width), bf16), ROWS),
            (shape((1, width), f32), None),
        ],
        18 * tokens * width * width,
    )
    grad_projected, *terms = lax.optimization_barrier(
        (grad_projected, *[total for total, _ in begun])
    )
    sums = [
        summed(term, "seq", 1, halved).astype(f32) for term, (_, halved) in zip(terms, begun)
    ]
    grad_w_qkv = mm(normed, grad_projected, TN)
    output, input_grad = output[None], input_grad[None]
    owners = lax.axis_size("wshard")
    gains = reduced(
        jnp.stack([grad_gain_a.reshape(owners, -1), grad_gain_m.reshape(owners, -1)], axis=1),
        "wshard",
        "seq",
    )
    return (
        output,
        input_grad,
        gains[0],
        total_of(term_of(grad_w_qkv)),
        sums[2],
        gains[1],
        sums[0],
        sums[1],
    )


def solution(mesh):
    return jax.shard_map(
        local,
        mesh=mesh,
        in_specs=(
            P("wshard", "seq", None),
            P("wshard"),
            P("wshard", None),
            P("wshard", None),
            P("wshard"),
            P("wshard", None),
            P("wshard", None),
            P("wshard", None),
            P("wshard", "seq", None),
        ),
        out_specs=(
            P("wshard", "seq", None),
            P("wshard", "seq", None),
            P("wshard"),
            P("wshard", None),
            P("wshard", None),
            P("wshard"),
            P("wshard", None),
            P("wshard", None),
        ),
        check_vma=False,
    )
```

```python
import functools
import math

import jax
import jax.numpy as jnp
from jax import lax
from jax.experimental import pallas as pl
from jax.experimental.pallas import tpu as pltpu
from jax.sharding import PartitionSpec as P

HD = 64
HALF = 64


rope_base = 10000.0


def extended_2(shard, sides, width):
    for axis, dim in sides:
        size, length = (lax.axis_size(axis), shard.shape[dim])
        up = [(i, (i + 1) % size) for i in range(size - 1)]
        down = [(j, i) for i, j in up]
        last = lax.slice_in_dim(shard, length - width, length, axis=dim)
        leading = lax.slice_in_dim(shard, 0, width, axis=dim)
        before = lax.ppermute(last, axis, up)
        after = lax.ppermute(leading, axis, down)
        shard = jnp.concatenate([before, shard, after], axis=dim)
    return shard


def from_behind(shard, axis, by):
    size = lax.axis_size(axis)
    pairs = [(i, i + by) for i in range(size) if 0 <= i + by < size]
    return lax.ppermute(shard, axis, pairs)


def swap(shard, axis, bit):
    return lax.ppermute(shard, axis, [(i, i ^ bit) for i in range(lax.axis_size(axis))])


def bits_of(axis):
    return [1 << b for b in range(lax.axis_size(axis).bit_length() - 1)]


def gathered_by_swaps(shard, axis):
    size, me = lax.axis_size(axis), lax.axis_index(axis)
    parts = shard[None]
    for bit in reversed(bits_of(axis)):
        other = swap(parts, axis, bit)
        upper = (me & bit) > 0
        parts = jnp.stack(
            [jnp.where(upper, other, parts), jnp.where(upper, parts, other)], axis=1
        ).reshape((-1,) + shard.shape)
    return parts.reshape((size * shard.shape[0],) + shard.shape[1:])


def owner_step(term, axis, bit):
    side = ((lax.axis_index(axis) & bit) > 0).astype(jnp.int32)
    pairs = term.reshape((term.shape[0] // 2, 2) + term.shape[1:])
    kept = lax.dynamic_index_in_dim(pairs, side, 1, keepdims=False)
    sent = lax.dynamic_index_in_dim(pairs, 1 - side, 1, keepdims=False)
    return kept + swap(sent, axis, bit)


def sum_step(total, axis, bit, halved):
    rows = total.shape[0]
    if bit == bits_of(axis)[-1] or rows % 16:
        return total + swap(total, axis, bit), halved
    side = ((lax.axis_index(axis) & bit) > 0).astype(jnp.int32)
    kept = lax.dynamic_slice_in_dim(total, side * (rows // 2), rows // 2, 0)
    sent = lax.dynamic_slice_in_dim(total, (1 - side) * (rows // 2), rows // 2, 0)
    return kept + swap(sent, axis, bit), halved + [bit]


def summed(total, axis, done=0, halved=()):
    halved = list(halved)
    for bit in bits_of(axis)[done:]:
        total, halved = sum_step(total, axis, bit, halved)
    for bit in reversed(halved):
        other = swap(total, axis, bit)
        upper = (lax.axis_index(axis) & bit) > 0
        total = jnp.concatenate(
            [jnp.where(upper, other, total), jnp.where(upper, total, other)], axis=0
        )
    return total


def reduced(term, owner_axis, sum_axis):
    while term.shape[0] > 1:
        bit = lax.axis_size(owner_axis) // term.shape[0]
        term = owner_step(term, owner_axis, bit)
    return summed(term[0], sum_axis)


def term_of(grad):
    owners = lax.axis_size("wshard")
    return grad.astype(jnp.bfloat16).reshape(owners, grad.shape[0] // owners, grad.shape[1])


def folded(term, columns):
    times = columns // term.shape[2]
    rows = term.shape[1] // times
    parts = [term[:, j * rows : (j + 1) * rows] for j in range(times)]
    return jnp.concatenate(parts, axis=2)


def unfolded(total, columns):
    return jnp.concatenate(
        [total[:, j : j + columns] for j in range(0, total.shape[1], columns)], axis=0
    )


def total_of(term):
    return reduced(term, "wshard", "seq").astype(jnp.float32)


def rope_tables(positions, head_dim):
    frequency = rope_base ** (-(jnp.arange(head_dim // 2, dtype=jnp.float32) * 2.0) / head_dim)
    angles = positions[:, None] * frequency[None, :]
    return (jnp.cos(angles)[:, None, :], jnp.sin(angles)[:, None, :])


ROWS = 256
QROWS = 128
LANES = 128
VMEM = 52 * 1024 * 1024
NT = (((1,), (1,)), ((), ()))
TN = (((0,), (0,)), ((), ()))


def mm(a, b, dims=(((1,), (0,)), ((), ()))):
    return lax.dot_general(a, b, dims, preferred_element_type=jnp.float32)


def standardised(stream):
    centred = stream - jnp.mean(stream, axis=-1, keepdims=True)
    scale = lax.rsqrt(jnp.mean(centred * centred, axis=-1, keepdims=True) + 1e-05)
    return centred * scale, scale


def norm_back(grad, unit, scale, gain):
    scaled = grad * gain
    first = jnp.mean(scaled, axis=-1, keepdims=True)
    second = jnp.mean(scaled * unit, axis=-1, keepdims=True)
    return scale * (scaled - first - unit * second)


def turn(chunk, cosine, sine_low, sine_high):
    ahead = pltpu.roll(chunk, LANES - HD // 2, 1)
    behind = pltpu.roll(chunk, HD // 2, 1)
    return chunk * cosine + ahead * sine_low + behind * sine_high


def qkv_kernel(x_ref, gain_ref, w_ref, cos_ref, low_ref, high_ref, normed_ref, q_ref, kv_ref):
    width = x_ref.shape[1]
    unit, _ = standardised(x_ref[...].astype(jnp.float32))
    normed = (unit * gain_ref[...]).astype(jnp.bfloat16)
    normed_ref[...] = normed
    cosine, low, high = cos_ref[...], low_ref[...], high_ref[...]
    for part in range(3):
        block = mm(normed, w_ref[:, part * width : (part + 1) * width])
        for c in range(0, width, LANES):
            chunk = block[:, c : c + LANES]
            if part < 2:
                chunk = turn(chunk, cosine, low, high)
            chunk = chunk.astype(jnp.bfloat16)
            if part == 0:
                q_ref[:, c : c + LANES] = chunk
            else:
                base = (part - 1) * width + c
                kv_ref[:, base : base + LANES] = chunk


def band_mask(meta_ref):
    start = meta_ref[2] + pl.program_id(0) * QROWS
    shape = (QROWS, QROWS + 2 * HALF)
    row = lax.broadcasted_iota(jnp.int32, shape, 0)
    col = lax.broadcasted_iota(jnp.int32, shape, 1)
    query_pos = start + row
    key_pos = start - HALF + col
    cut_first, cut_last = meta_ref[0], meta_ref[1]

    def segment(at):
        return (at >= cut_first).astype(jnp.int32) + (at >= cut_last).astype(jnp.int32)

    near = jnp.abs(query_pos - key_pos) <= HALF
    inside = (key_pos >= 0) & (key_pos < meta_ref[3])
    return near & inside & (segment(query_pos) == segment(key_pos))


def lower_lanes(rows):
    return lax.broadcasted_iota(jnp.int32, (rows, LANES), 1) < HD


def attend_kernel(meta_ref, q_ref, kv_ref, out_ref, lse_ref):
    width = q_ref.shape[1]
    allowed = band_mask(meta_ref)
    lower = lower_lanes(QROWS)
    rows = pl.ds(pl.multiple_of(pl.program_id(0) * QROWS, QROWS), QROWS + 2 * HALF)
    scale = 1.0 / math.sqrt(HD)
    lane = lax.broadcasted_iota(jnp.int32, (QROWS, LANES), 1)
    lses = jnp.zeros((QROWS, LANES), jnp.float32)
    for c in range(0, width, LANES):
        q = q_ref[:, c : c + LANES]
        k = kv_ref[rows, c : c + LANES]
        v = kv_ref[rows, width + c : width + c + LANES]
        outs = []
        for half in range(2):
            mine = lower if half == 0 else jnp.logical_not(lower)
            scores = mm(jnp.where(mine, q, jnp.zeros_like(q)), k, NT) * scale
            scores = jnp.where(allowed, scores, -1e30)
            top = jnp.max(scores, axis=-1, keepdims=True)
            expo = jnp.exp(scores - top)
            total = jnp.sum(expo, axis=-1, keepdims=True)
            probs = (expo * (1.0 / total)).astype(jnp.bfloat16)
            outs.append(mm(probs, v))
            lses = jnp.where(lane == c // HD + half, top + jnp.log(total), lses)
        out_ref[:, c : c + LANES] = jnp.where(lower, outs[0], outs[1]).astype(jnp.bfloat16)
    lse_ref[...] = lses


def attend_back_kernel(
    group, meta_ref, q_ref, go_ref, k_ref, v_ref, lse_ref, cos_ref, low_ref, high_ref,
    dq_ref, dk_ref, dv_ref,
):
    width = q_ref.shape[1]

    @pl.when(pl.program_id(0) == 0)
    def _():
        dk_ref[...] = jnp.zeros_like(dk_ref)
        dv_ref[...] = jnp.zeros_like(dv_ref)

    allowed = band_mask(meta_ref)
    lower = lower_lanes(QROWS)
    rows = pl.ds(pl.multiple_of(pl.program_id(0) * QROWS, QROWS), QROWS + 2 * HALF)
    scale = 1.0 / math.sqrt(HD)
    for c in range(0, width, LANES):
        q = q_ref[:, c : c + LANES]
        go = go_ref[:, c : c + LANES]
        k = k_ref[rows, c : c + LANES]
        v = v_ref[rows, c : c + LANES]
        dqs = []
        dk = dv = None
        for half in range(2):
            mine = lower if half == 0 else jnp.logical_not(lower)
            q_half = jnp.where(mine, q, jnp.zeros_like(q))
            go_half = jnp.where(mine, go, jnp.zeros_like(go))
            head = (group * width + c) // HD + half
            scores = mm(q_half, k, NT) * scale
            scores = jnp.where(allowed, scores, -1e30)
            probs = jnp.exp(scores - lse_ref[:, head : head + 1])
            prob_grad = mm(go_half, v, NT)
            centre = jnp.sum(probs * prob_grad, axis=-1, keepdims=True)
            score_grad = (probs * (prob_grad - centre)).astype(jnp.bfloat16)
            dqs.append(mm(score_grad, k))
            dk_half = mm(score_grad, q_half, TN)
            dv_half = mm(probs.astype(jnp.bfloat16), go_half, TN)
            dk = dk_half if dk is None else dk + dk_half
            dv = dv_half if dv is None else dv + dv_half
        dq = (jnp.where(lower, dqs[0], dqs[1]) * scale).astype(jnp.bfloat16).astype(jnp.float32)
        dq_ref[:, c : c + LANES] = turn(
            dq, cos_ref[...], -low_ref[...], -high_ref[...]
        ).astype(jnp.bfloat16)
        dk_ref[rows, c : c + LANES] += dk * scale
        dv_ref[rows, c : c + LANES] += dv


def mlp_kernel(
    x_ref, att_ref, g_ref, gain_ref, wo_ref, wi_ref, wd_ref,
    out_ref, normed_ref, hidden_ref, gl_ref, gmid_ref, gm_ref, gatt_ref, ggain_ref,
):
    wide = wd_ref.shape[0]
    middle = x_ref[...].astype(jnp.float32) + mm(att_ref[...], wo_ref[...])
    unit, spread = standardised(middle)
    gain = gain_ref[...]
    normed = (unit * gain).astype(jnp.bfloat16)
    normed_ref[...] = normed
    active = mm(normed, wi_ref[:, :wide])
    gate = mm(normed, wi_ref[:, wide:])
    cdf = 0.5 * (1.0 + lax.erf(active * math.sqrt(0.5)))
    act = active * cdf
    hidden = (act * gate).astype(jnp.bfloat16)
    hidden_ref[...] = hidden
    out_ref[...] = (middle + mm(hidden, wd_ref[...])).astype(jnp.bfloat16)
    gd = g_ref[...]
    grad_hidden = mm(gd, wd_ref[...], NT)
    slope = cdf + active * (jnp.exp(-0.5 * active * active) * (1.0 / math.sqrt(2.0 * math.pi)))
    grad_active = (grad_hidden * gate * slope).astype(jnp.bfloat16)
    grad_gate = (grad_hidden * act).astype(jnp.bfloat16)
    gl_ref[:, :wide] = grad_active
    gl_ref[:, wide:] = grad_gate
    grad_normed = mm(grad_active, wi_ref[:, :wide], NT) + mm(grad_gate, wi_ref[:, wide:], NT)

    @pl.when(pl.program_id(0) == 0)
    def _():
        ggain_ref[...] = jnp.zeros_like(ggain_ref)

    ggain_ref[...] += jnp.sum(grad_normed * unit, axis=0, keepdims=True)
    grad_middle = gd.astype(jnp.float32) + norm_back(grad_normed, unit, spread, gain)
    gmid_ref[...] = grad_middle
    gm = grad_middle.astype(jnp.bfloat16)
    gm_ref[...] = gm
    gatt_ref[...] = mm(gm, wo_ref[...], NT).astype(jnp.bfloat16)


def last_kernel(
    x_ref, gain_ref, w_ref, dq0_ref, dq1_ref, dk0_ref, dk1_ref, dv0_ref, dv1_ref, prev_ref,
    next_ref, cos_ref, low_ref, high_ref, gmid_ref, gp_ref, out_ref, ggain_ref,
):
    width = x_ref.shape[1]
    step = pl.program_id(0)
    start = pl.multiple_of(step * ROWS + HALF, HALF)
    first = (step == 0).astype(jnp.float32)
    last = (step == pl.num_programs(0) - 1).astype(jnp.float32)
    part = width // 2
    gp_ref[:, :part] = dq0_ref[...]
    gp_ref[:, part:width] = dq1_ref[...]
    pieces = (dk0_ref, dk1_ref, dv0_ref, dv1_ref)
    for c in range(0, 2 * width, LANES):
        own = pieces[c // part][pl.ds(start, ROWS), c % part : c % part + LANES]
        top = own[:HALF] + prev_ref[:, c : c + LANES].astype(jnp.float32) * first
        low_end = own[ROWS - HALF :] + next_ref[:, c : c + LANES].astype(jnp.float32) * last
        chunk = jnp.concatenate([top, own[HALF : ROWS - HALF], low_end], axis=0)
        chunk = chunk.astype(jnp.bfloat16)
        if c < width:
            chunk = turn(
                chunk.astype(jnp.float32), cos_ref[...], -low_ref[...], -high_ref[...]
            ).astype(jnp.bfloat16)
        gp_ref[:, width + c : width + c + LANES] = chunk
    grad_normed = mm(gp_ref[...], w_ref[...], NT)
    unit, spread = standardised(x_ref[...].astype(jnp.float32))

    @pl.when(step == 0)
    def _():
        ggain_ref[...] = jnp.zeros_like(ggain_ref)

    ggain_ref[...] += jnp.sum(grad_normed * unit, axis=0, keepdims=True)
    out_ref[...] = (gmid_ref[...] + norm_back(grad_normed, unit, spread, gain_ref[...])).astype(
        jnp.bfloat16
    )


def run(body, steps, ins, outs, flops):
    def spec(array, rows):
        if isinstance(rows, tuple):
            rows, cols, place = rows
            if rows is None:
                return pl.BlockSpec((array.shape[0], cols), lambda i: (0, place))
            return pl.BlockSpec((rows, cols), lambda i: (i, place))
        if rows == 0:
            return pl.BlockSpec(memory_space=pltpu.SMEM)
        if rows is None:
            return pl.BlockSpec(array.shape, lambda i: (0, 0))
        return pl.BlockSpec((rows, array.shape[1]), lambda i: (i, 0))

    moved = sum(a.size * a.dtype.itemsize for a, _ in ins + outs)
    return pl.pallas_call(
        body,
        grid=(steps,),
        in_specs=[spec(a, r) for a, r in ins],
        out_specs=[spec(a, r) for a, r in outs],
        out_shape=[a for a, _ in outs],
        compiler_params=pltpu.CompilerParams(
            vmem_limit_bytes=VMEM, dimension_semantics=("arbitrary",)
        ),
        cost_estimate=pl.CostEstimate(
            flops=int(flops), bytes_accessed=int(moved), transcendentals=0
        ),
    )(*[a for a, _ in ins])


def local(inputs, gain_attn, w_qkv, w_out, gain_mlp, w_in, w_down, bounds, grad_out):
    tokens = inputs.shape[1]
    width = inputs.shape[2]
    length = tokens * lax.axis_size("seq")
    offset = lax.axis_index("seq") * tokens
    shape = jax.ShapeDtypeStruct
    bf16, f32 = jnp.bfloat16, jnp.float32
    gains_all = gathered_by_swaps(jnp.stack([gain_attn, gain_mlp], axis=1), "wshard")
    gain_a = gains_all[:, 0].astype(f32)[None]
    gain_m = gains_all[:, 1].astype(f32)[None]
    weight_qkv = lax.all_gather(w_qkv, "wshard", axis=0, tiled=True)
    weight_out = lax.all_gather(w_out, "wshard", axis=0, tiled=True)
    weight_qkv, w_in = lax.optimization_barrier((weight_qkv, w_in))
    weight_in = gathered_by_swaps(w_in, "wshard")
    weight_down = lax.all_gather(w_down, "wshard", axis=0, tiled=True)
    wide = weight_down.shape[0]
    stream = inputs[0]
    upstream = grad_out[0]
    positions = (offset + jnp.arange(tokens, dtype=jnp.int32)).astype(f32)
    cosine, sine = rope_tables(positions, HD)
    cosine, sine = cosine[:, 0], sine[:, 0]
    none = jnp.zeros_like(sine)
    cos_t = jnp.concatenate([cosine] * 4, axis=1)
    low_t = jnp.concatenate([-sine, none] * 2, axis=1)
    high_t = jnp.concatenate([none, sine] * 2, axis=1)
    steps, qsteps = tokens // ROWS, tokens // QROWS
    normed, query, kv = run(
        qkv_kernel,
        steps,
        [(stream, ROWS), (gain_a, None), (weight_qkv, None)]
        + [(cos_t, ROWS), (low_t, ROWS), (high_t, ROWS)],
        [
            (shape((tokens, width), bf16), ROWS),
            (shape((tokens, width), bf16), ROWS),
            (shape((tokens, 2 * width), bf16), ROWS),
        ],
        18 * tokens * width * width,
    )
    kv_ext = extended_2(kv, (("seq", 0),), HALF)
    meta = jnp.stack([bounds[0, 0], bounds[0, 1], offset, jnp.int32(length)]).astype(jnp.int32)
    attended, lse = run(
        attend_kernel,
        qsteps,
        [(meta, 0), (query, QROWS), (kv_ext, None)],
        [(shape((tokens, width), bf16), QROWS), (shape((tokens, LANES), f32), QROWS)],
        150 * tokens * width * QROWS,
    )
    output, normed2, hidden, grad_lifted, grad_middle, grad_mid_low, grad_att, grad_gain_m = run(
        mlp_kernel,
        steps,
        [(stream, ROWS), (attended, ROWS), (upstream, ROWS), (gain_m, None)]
        + [(weight_out, None), (weight_in, None), (weight_down, None)],
        [
            (shape((tokens, width), bf16), ROWS),
            (shape((tokens, width), bf16), ROWS),
            (shape((tokens, wide), bf16), ROWS),
            (shape((tokens, 2 * wide), bf16), ROWS),
            (shape((tokens, width), f32), ROWS),
            (shape((tokens, width), bf16), ROWS),
            (shape((tokens, width), bf16), ROWS),
            (shape((1, width), f32), None),
        ],
        4 * tokens * width * (width + 3 * wide),
    )
    term_in = term_of(mm(normed2, grad_lifted, TN))
    term_down = folded(term_of(mm(hidden, upstream, TN)), 2 * wide)
    term_out = folded(term_of(mm(attended, grad_mid_low, TN)), 2 * wide)
    in_rows, down_rows = term_in.shape[1], term_down.shape[1]
    terms = [jnp.concatenate([term_in, term_down, term_out], axis=1)]
    grad_att, *terms = lax.optimization_barrier((grad_att, *terms))
    part = width // 2
    query_grads, key_grads, value_grads = [], [], []
    for group in range(2):
        dq, dk, dv = run(
            functools.partial(attend_back_kernel, group),
            qsteps,
            [(meta, 0), (query, (QROWS, part, group)), (grad_att, (QROWS, part, group))]
            + [(kv_ext, (None, part, group)), (kv_ext, (None, part, 2 + group)), (lse, QROWS)]
            + [(cos_t, QROWS), (low_t, QROWS), (high_t, QROWS)],
            [(shape((tokens, part), bf16), QROWS)]
            + [(shape((tokens + 2 * HALF, part), f32), None)] * 2,
            200 * tokens * width * QROWS,
        )
        query_grads.append(dq)
        key_grads.append(dk)
        value_grads.append(dv)
        if group == 0:
            terms = [owner_step(term, "wshard", 1) for term in terms]
            dq, grad_att, *terms = lax.optimization_barrier((dq, grad_att, *terms))
            query_grads[0] = dq
    pieces = key_grads + value_grads
    from_next = from_behind(
        jnp.concatenate([piece[:HALF] for piece in pieces], axis=1).astype(bf16), "seq", -1
    )
    from_prev = from_behind(
        jnp.concatenate([piece[tokens + HALF :] for piece in pieces], axis=1).astype(bf16), "seq", 1
    )
    terms = [owner_step(term, "wshard", 2)[0] for term in terms]
    from_next, from_prev, *terms = lax.optimization_barrier((from_next, from_prev, *terms))
    begun = [sum_step(term, "seq", 1, []) for term in terms]
    grad_projected, input_grad, grad_gain_a = run(
        last_kernel,
        steps,
        [(stream, ROWS), (gain_a, None), (weight_qkv, None), (query_grads[0], ROWS)]
        + [(query_grads[1], ROWS)]
        + [(piece, None) for piece in pieces]
        + [(from_prev, None), (from_next, None)]
        + [(cos_t, ROWS), (low_t, ROWS), (high_t, ROWS), (grad_middle, ROWS)],
        [
            (shape((tokens, 3 * width), bf16), ROWS),
            (shape((tokens, width), bf16), ROWS),
            (shape((1, width), f32), None),
        ],
        18 * tokens * width * width,
    )
    grad_projected, *terms = lax.optimization_barrier(
        (grad_projected, *[total for total, _ in begun])
    )
    sums = [
        summed(term, "seq", 1, halved).astype(f32) for term, (_, halved) in zip(terms, begun)
    ]
    sum_in = sums[0][:in_rows]
    sum_down = unfolded(sums[0][in_rows : in_rows + down_rows], width)
    sum_out = unfolded(sums[0][in_rows + down_rows :], width)
    grad_w_qkv = mm(normed, grad_projected, TN)
    output, input_grad = output[None], input_grad[None]
    owners = lax.axis_size("wshard")
    gains = reduced(
        jnp.stack([grad_gain_a.reshape(owners, -1), grad_gain_m.reshape(owners, -1)], axis=1),
        "wshard",
        "seq",
    )
    return (
        output,
        input_grad,
        gains[0],
        total_of(term_of(grad_w_qkv)),
        sum_out,
        gains[1],
        sum_in,
        sum_down,
    )


def solution(mesh):
    return jax.shard_map(
        local,
        mesh=mesh,
        in_specs=(
            P("wshard", "seq", None),
            P("wshard"),
            P("wshard", None),
            P("wshard", None),
            P("wshard"),
            P("wshard", None),
            P("wshard", None),
            P("wshard", None),
            P("wshard", "seq", None),
        ),
        out_specs=(
            P("wshard", "seq", None),
            P("wshard", "seq", None),
            P("wshard"),
            P("wshard", None),
            P("wshard", None),
            P("wshard"),
            P("wshard", None),
            P("wshard", None),
        ),
        check_vma=False,
    )
```
